32 devices in a mesh: groups: 2 (over y), dp: 4 (over x, core), expert: 4 (over z).
Axes of the slice: x: 2, y: 2, z: 4, core: 2. Of those that a mesh axis runs over, the one named last changes fastest.
Arguments:
- tokens: bfloat16 [2, 64, 7168], P(None, ('groups', 'dp', 'expert')), parts along dimension 1, may hold values from -6 to 6
- expert_ids: int32 [2, 64, 2], P(None, ('groups', 'dp', 'expert')), parts along dimension 1, may hold values from 0 to 3, all different within a row; in each aligned block of 2 rows (0 to 1, 2 to 3, ..., all dimensions but the last counted through in order) at most 2 rows name the same one
- router_weight: bfloat16 [7168, 4], replicated, may hold values from -0.0625 to 0.0625
- w_in: bfloat16 [7168, 2, 8192], P('dp', None, 'expert'), may hold values from -0.0625 to 0.0625
- w_down: bfloat16 [8192, 7168], P('expert', 'dp'), may hold values from -0.125 to 0.125
Outputs:
- combined: bfloat16 [2, 64, 7168], P(None, ('groups', 'dp', 'expert')), parts along dimension 1
The draws below stay inside these ranges and needn't reach their ends.
There are 2 independent parts, one for each index of `groups`. The reference program is written for one: setup_inputs(seed, part) draws one part's arguments, and reference() takes and returns one part's arrays. A program takes and returns all parts, laid end to end along the dimension named above; an argument that names none is the same for every part. Nothing has to cross between parts.
Inputs may be any that keep to these rules, and one draw needn't show every extreme that they name: `expert_ids`: each token names 2 different experts. Within the 2 tokens of one device in one micro-batch (aligned blocks of rows, micro-batch major), no expert is named by more than 2 tokens, a bound that some block reaches.
All inputs are finite; a program needn't handle non-finite values.
Results may differ from the reference program's by a relative error of at most 0.02.
Values may be sent and summed in bfloat16 or wider, within the bound.
A program may use at most 128 MiB of HBM per device.

```python
import math
import jax
import jax.numpy as jnp
import numpy as np
from jax import lax

D = 7168
FF = 2048
MB = 2
TOK_MB = 2
EXPERTS = 4
SPLIT = 1
TOP = 2
CAP = 2
TOKENS = 32


def level_of(key, dims, cuts, low, largest):
    factor_of = 1.0
    for position, blocks in cuts:
        steps = jax.random.uniform(jax.random.fold_in(jax.random.fold_in(key, 6), position), (blocks,), jnp.float32, low / len(cuts), largest / len(cuts))
        factor_of = factor_of * jnp.repeat(jnp.exp(steps), dims[position] // blocks).reshape((-1,) + (1,) * (len(dims) - 1 - position))
    return factor_of


def shared_out(stream_key, own, number, rows, number_of, top, bound, skew):
    order = jax.random.permutation(stream_key, number_of)
    crowded, usual = shares(number_of, rows * top, bound, skew, True), shares(number_of, rows * top, bound, skew, False)
    places = jnp.arange(number_of)

    def named(tallies, rotation):
        used = int((tallies > 0).sum())
        fixed = max(1, used // 4)
        shifted = fixed + (places - fixed + rotation * (used - fixed)) % max(1, number_of - fixed)
        return jnp.zeros((number_of,), jnp.int32).at[order[jnp.where(places < fixed, places, shifted)]].set(jnp.asarray(tallies, jnp.int32))

    tallies = jnp.where(number % 4 == 0, named(crowded, number // 4), named(usual, number - number // 4 - 1))
    mixed = jax.random.permutation(jax.random.fold_in(own, 3), number_of)
    giver, receiver = mixed[0:number_of // 2 * 2:2], mixed[1:number_of // 2 * 2:2]
    slack = jnp.minimum(tallies[giver] - 1, bound - tallies[receiver]) // 2
    slack = jnp.where((giver == order[0]) | (receiver == order[0]) | (tallies[receiver] == 0), 0, jnp.maximum(slack, 0))
    shifted = jax.random.randint(jax.random.fold_in(own, 4), (number_of // 2,), 0, 1 << 20) % (slack + 1)
    tallies = tallies.at[giver].add(-shifted).at[receiver].add(shifted)
    items = jnp.searchsorted(jnp.cumsum(tallies), jnp.arange(rows * top), side="right").astype(jnp.int32)
    table = items.reshape(top, rows).T
    table = table[jax.random.permutation(jax.random.fold_in(own, 1), rows)]
    rotation = jax.random.randint(jax.random.fold_in(own, 2), (rows, 1), 0, top)
    return jnp.take_along_axis(table, (jnp.arange(top)[None, :] + rotation) % top, axis=1)


def shares(count, total, reach, skew, full):
    portions = [(1 << 20) // math.isqrt(standing ** skew) + 1 for standing in range(1, count + 1)]
    largest = reach if full else min(reach, max(-(-total // count), total * portions[0] // sum(portions)))
    least = 1 if total - largest >= count - 1 else 0
    holding, spare = [largest] + [least] * (count - 1), total - largest - least * (count - 1)
    while spare > 0:
        movable = [i for i in range(1, count) if holding[i] < largest] or [i for i in range(1, count) if holding[i] < reach]
        whole, remaining = sum([portions[i] for i in movable]), spare
        for i in movable:
            addition = min(reach - holding[i], max(1, remaining * portions[i] // whole), spare)
            holding[i] = holding[i] + addition
            spare = spare - addition
    return np.array(holding)


def scatter_about(stream_key, shape, scale, bound, split=(), kind=jnp.bfloat16):
    array = scale * jax.random.normal(stream_key, shape, jnp.float32)
    if split:
        array = array * level_of(stream_key, shape, split, -0.22, 0.18)
    return jnp.clip(array, -bound, bound).astype(kind)


def setup_inputs(seed: int = 0, part: int = 0) -> dict:
    key_of = jax.random.split(jax.random.key(seed), 6)
    part_keys = jax.random.split(jax.random.fold_in(key_of[5], part), 6)
    tokens = scatter_about(part_keys[0], (MB, TOKENS, D), 1.0, 6.0, ((1, 16),))
    expert_ids_keys = jax.random.split(jax.random.fold_in(part_keys[1], 1), MB * TOKENS // TOK_MB)
    expert_ids_turns = jax.random.permutation(jax.random.fold_in(part_keys[1], 3), MB * TOKENS // TOK_MB)
    expert_ids = jax.vmap(lambda own, number: shared_out(jax.random.fold_in(part_keys[1], 2), own, number, TOK_MB, EXPERTS, TOP, CAP, 2))(expert_ids_keys, expert_ids_turns).reshape((MB, TOKENS, TOP))
    router_weight = scatter_about(key_of[2], (D, EXPERTS), D ** -0.5, 0.0625)
    w_in = scatter_about(key_of[3], (D, 2, EXPERTS * FF), D ** -0.5, 0.0625, ((0, 4), (2, 4)))
    w_down = scatter_about(key_of[4], (EXPERTS * FF, D), FF ** -0.5, 0.125, ((0, 4), (1, 4)))
    return {"tokens": tokens, "expert_ids": expert_ids, "router_weight": router_weight, "w_in": w_in, "w_down": w_down}


route_scale = 2.5


def gate_values(tokens, expert_ids, router_weight):
    logits = jnp.einsum('mtd,de->mte', tokens.astype(jnp.float32), router_weight.astype(jnp.float32))
    scores = jax.nn.sigmoid(logits)
    chosen = jnp.take_along_axis(scores, expert_ids, axis=2)
    return route_scale * chosen / jnp.sum(chosen, axis=2, keepdims=True)


def reference(tokens, expert_ids, router_weight, w_in, w_down):
    num_rows = MB * TOKENS
    block_units = FF // SPLIT
    flat_tokens = tokens.reshape(num_rows, D)
    flat_ids = expert_ids.reshape(num_rows, TOP)
    flat_gates = gate_values(tokens, expert_ids, router_weight).reshape(num_rows, TOP)

    def per_expert(summed, expert):
        weight_row = jnp.sum(jnp.where(flat_ids == expert, flat_gates, 0.0), axis=1)
        w_first = lax.dynamic_slice_in_dim(w_in, (expert * FF).astype(jnp.int32), FF, 2)
        w_second = lax.dynamic_slice_in_dim(w_down, (expert * FF).astype(jnp.int32), FF, 0)
        gate = jnp.dot(flat_tokens, w_first[:, 0, :], preferred_element_type=jnp.float32)
        up = jnp.dot(flat_tokens, w_first[:, 1, :], preferred_element_type=jnp.float32)
        hidden = (jax.nn.silu(gate) * up).astype(jnp.bfloat16)
        hidden_blocks = hidden.reshape(num_rows, SPLIT, block_units).astype(jnp.float32)
        down_blocks = w_second.reshape(SPLIT, block_units, D).astype(jnp.float32)
        part_out = jnp.einsum('rjf,jfd->rjd', hidden_blocks, down_blocks).astype(jnp.bfloat16)
        result = jnp.sum(part_out.astype(jnp.float32), axis=1).astype(jnp.bfloat16)
        summed = summed + weight_row[:, None] * result.astype(summed.dtype)
        return summed, None

    summed = jnp.zeros((num_rows, D), jnp.float32)
    summed = lax.scan(per_expert, summed, jnp.arange(EXPERTS, dtype=jnp.int32))[0]
    return summed.reshape(MB, TOKENS, D).astype(jnp.bfloat16)
```

```python
import functools
import jax
import jax.numpy as jnp
from jax import lax
from jax.experimental import pallas as pl
from jax.experimental.pallas import tpu as pltpu
from jax.sharding import PartitionSpec as P

route_scale = 2.5
f32 = jnp.float32
bf16 = jnp.bfloat16


def loop(count, step):
    if count <= 32:
        for i in range(count):
            step(i)
    else:
        lax.fori_loop(0, count, lambda i, c: (step(i), c)[1], 0)


def kernel(n_dp, n_exp, ids, tok, rw, w_in, w_down, out, stage, xin, lhs, wv, dv, rs_out, rs_in,
           h_all, acc, o_stage, ret, w_sem, d_sem, x_send, x_recv, rs_send, rs_recv, h_send,
           h_recv, o_send, o_recv):
    num_micro, tok_rows, width = tok.shape
    top = ids.shape[2]
    experts = rw.shape[0]
    sharers = n_exp // experts
    quarter = width // n_dp
    per_dev = num_micro * tok_rows
    peers = n_dp * n_exp
    rows = peers * per_dev
    share = rows // n_dp
    chunks, _, cw = wv.shape
    my_d = lax.axis_index("dp")
    my_z = lax.axis_index("expert")
    me = my_d * n_exp + my_z

    def w_copy(c):
        src = w_in.reshape(2 * quarter, chunks * cw)
        return pltpu.make_async_copy(src.at[:, pl.ds(c * cw, cw)], wv.at[c], w_sem.at[c])

    def d_copy(c):
        return pltpu.make_async_copy(w_down.at[pl.ds(c * cw, cw)], dv.at[c], d_sem.at[c])

    barrier = pltpu.get_barrier_semaphore()

    def peer_of(i):
        p = lax.rem(me + 1 + i, peers)
        return p, p // n_exp, lax.rem(p, n_exp)

    def greet(i):
        _, q, z = peer_of(i)
        pl.semaphore_signal(barrier, inc=1, device_id={"dp": q, "expert": z},
                            device_id_type=pl.DeviceIdType.MESH)

    loop(peers - 1, greet)
    for c in range(chunks):
        w_copy(c).start()
    for c in range(chunks):
        d_copy(c).start()
    mine = jnp.concatenate([tok[m].astype(f32) for m in range(num_micro)], axis=0)
    mine16 = mine.astype(bf16)
    for q in range(n_dp):
        stage[q] = mine16[:, q * quarter:(q + 1) * quarter]
    pl.semaphore_wait(barrier, peers - 1)

    def x_send_to(i):
        _, q, z = peer_of(i)
        pltpu.make_async_remote_copy(
            src_ref=stage.at[q], dst_ref=xin.at[me], send_sem=x_send, recv_sem=x_recv,
            device_id={"dp": q, "expert": z}, device_id_type=pl.DeviceIdType.MESH).start()

    loop(peers - 1, x_send_to)
    xin[me] = stage[my_d]
    logits = lax.dot_general(mine16, rw[...], (((1,), (1,)), ((), ())), preferred_element_type=f32)
    scores = 1.0 / (1.0 + jnp.exp(-logits))
    row = lax.broadcasted_iota(jnp.int32, (per_dev, experts), 0)
    col = lax.broadcasted_iota(jnp.int32, (per_dev, experts), 1)
    picked = jnp.zeros((per_dev, experts), f32)
    for m in range(num_micro):
        for t in range(tok_rows):
            for k in range(top):
                hit = (row == m * tok_rows + t) & (col == ids[m, t, k])
                picked = picked + jnp.where(hit, 1.0, 0.0)
    chosen = scores * picked
    gates = route_scale * chosen / jnp.sum(chosen, axis=1, keepdims=True)

    all_but_one = xin.at[pl.ds(0, peers - 1)]
    pltpu.make_async_copy(all_but_one, all_but_one, x_recv).wait()
    r_i = lax.broadcasted_iota(jnp.int32, (128, 256), 0)
    c_i = lax.broadcasted_iota(jnp.int32, (128, 256), 1)
    even = jnp.where(c_i == 2 * r_i, 1.0, 0.0).astype(bf16)
    odd = jnp.where(c_i == 2 * r_i + 1, 1.0, 0.0).astype(bf16)
    block = min(rows, 64)
    group = block // per_dev

    def expand(b):
        x = jnp.concatenate([xin[b * group + k].astype(f32) for k in range(group)], axis=0)
        x = x.astype(bf16)
        for j in range(quarter // 128):
            piece = x[:, j * 128:(j + 1) * 128]
            for s, spread in enumerate((even, odd)):
                lhs[s, pl.ds(b * block, block), pl.ds(j * 256, 256)] = jnp.dot(
                    piece, spread, preferred_element_type=f32).astype(bf16)

    if rows == block:
        expand(0)
    else:
        lax.fori_loop(0, rows // block, lambda b, c: (expand(b), c)[1], 0)

    def up_chunk(c):
        w_copy(c).wait()
        if rows <= 64:
            res = jnp.dot(lhs[...].reshape(2 * rows, 2 * quarter), wv[c],
                          preferred_element_type=f32).astype(bf16)
            rs_out[c] = res.reshape(2, rows, cw)
        else:
            def part(b, carry):
                at = pl.ds(pl.multiple_of(b * block, block), block)
                for s in range(2):
                    rs_out[c, s, at] = jnp.dot(lhs[s, at], wv[c],
                                               preferred_element_type=f32).astype(bf16)
                return carry
            lax.fori_loop(0, rows // block, part, 0)
        for o in range(1, n_dp):
            t = lax.rem(my_d + o, n_dp)
            pltpu.make_async_remote_copy(
                src_ref=rs_out.at[c, :, pl.ds(pl.multiple_of(t * share, share), share)],
                dst_ref=rs_in.at[c, n_dp - 1 - o], send_sem=rs_send, recv_sem=rs_recv.at[c],
                device_id={"dp": t}, device_id_type=pl.DeviceIdType.MESH).start()

    def hidden_chunk(c):
        pltpu.make_async_copy(rs_in.at[c], rs_in.at[c], rs_recv.at[c]).wait()
        at = pl.ds(pl.multiple_of(my_d * share, share), share)
        total = rs_out[c, :, at].astype(f32)
        for o in range(n_dp - 1):
            total = total + rs_in[c, o].astype(f32)
        gate, up = total[0], total[1]
        h_all[c, my_d] = (gate / (1.0 + jnp.exp(-gate)) * up).astype(bf16)
        for o in range(1, n_dp):
            t = lax.rem(my_d + o, n_dp)
            pltpu.make_async_remote_copy(
                src_ref=h_all.at[c, my_d], dst_ref=h_all.at[c, my_d], send_sem=h_send,
                recv_sem=h_recv.at[c], device_id={"dp": t},
                device_id_type=pl.DeviceIdType.MESH).start()

    def down_chunk(c):
        d_copy(c).wait()
        others = h_all.at[c, pl.ds(0, n_dp - 1)]
        pltpu.make_async_copy(others, others, h_recv.at[c]).wait()
        if rows <= 64:
            part = jnp.dot(h_all[c].reshape(rows, cw), dv[c], preferred_element_type=f32)
            acc[...] = part if c == 0 else acc[...] + part
        else:
            per = share // block

            def part(b, carry):
                src = pl.ds(pl.multiple_of(lax.rem(b, per) * block, block), block)
                at = pl.ds(pl.multiple_of(b * block, block), block)
                value = jnp.dot(h_all[c, b // per, src], dv[c], preferred_element_type=f32)
                acc[at] = value if c == 0 else acc[at] + value
                return carry
            lax.fori_loop(0, rows // block, part, 0)

    lag_h, lag_d = 2, 4
    for step in range(chunks + lag_d):
        if step < chunks:
            up_chunk(step)
        if 0 <= step - lag_h < chunks:
            hidden_chunk(step - lag_h)
        if 0 <= step - lag_d < chunks:
            down_chunk(step - lag_d)

    def spread_out(i):
        v = acc[pl.ds(i * 16, 16), :]
        for k in range(16 // per_dev):
            o_stage[i * (16 // per_dev) + k] = v[k * per_dev:(k + 1) * per_dev].astype(bf16)

    loop(rows // 16, spread_out)

    def o_send_to(i):
        p, q, z = peer_of(i)
        pltpu.make_async_remote_copy(
            src_ref=o_stage.at[p], dst_ref=ret.at[me], send_sem=o_send, recv_sem=o_recv,
            device_id={"dp": q, "expert": z}, device_id_type=pl.DeviceIdType.MESH).start()

    loop(peers - 1, o_send_to)
    ret[me] = o_stage[me]
    back = ret.at[pl.ds(0, peers - 1)]
    pltpu.make_async_copy(back, back, o_recv).wait()
    for q in range(n_dp):
        total = jnp.zeros((per_dev, quarter), f32)
        for e in range(experts):
            part = ret[q * n_exp + e * sharers].astype(f32)
            for s in range(1, sharers):
                part = part + ret[q * n_exp + e * sharers + s].astype(f32)
            total = total + gates[:, e:e + 1] * part
        done = total.astype(bf16)
        for m in range(num_micro):
            out[m, :, pl.ds(q * quarter, quarter)] = total[
                m * tok_rows:(m + 1) * tok_rows].astype(bf16)
    pltpu.make_async_copy(all_but_one, all_but_one, x_send).wait()
    pltpu.make_async_copy(rs_in, rs_in, rs_send).wait()
    sent = h_all.at[:, pl.ds(0, n_dp - 1)]
    pltpu.make_async_copy(sent, sent, h_send).wait()
    pltpu.make_async_copy(back, back, o_send).wait()


def body(n_dp, n_exp, tokens, expert_ids, router_weight, w_in, w_down):
    num_micro, tok_rows, width = tokens.shape
    quarter, _, ff = w_in.shape
    per_dev = num_micro * tok_rows
    peers = n_dp * n_exp
    rows = peers * per_dev
    share = rows // n_dp
    cw = min(256, ff)
    chunks = ff // cw
    vmem = pl.BlockSpec(memory_space=pltpu.VMEM)
    dma = pltpu.SemaphoreType.DMA
    return pl.pallas_call(
        functools.partial(kernel, n_dp, n_exp),
        out_shape=jax.ShapeDtypeStruct(tokens.shape, bf16),
        in_specs=[pl.BlockSpec(memory_space=pltpu.SMEM), vmem, vmem,
                  pl.BlockSpec(memory_space=pl.ANY), pl.BlockSpec(memory_space=pl.ANY)],
        out_specs=vmem,
        scratch_shapes=[
            pltpu.VMEM((n_dp, per_dev, quarter), bf16),
            pltpu.VMEM((peers, per_dev, quarter), bf16),
            pltpu.VMEM((2, rows, 2 * quarter), bf16),
            pltpu.VMEM((chunks, 2 * quarter, cw), bf16),
            pltpu.VMEM((chunks, cw, quarter), bf16),
            pltpu.VMEM((chunks, 2, rows, cw), bf16),
            pltpu.VMEM((chunks, n_dp - 1, 2, share, cw), bf16),
            pltpu.VMEM((chunks, n_dp, share, cw), bf16),
            pltpu.VMEM((rows, quarter), f32),
            pltpu.VMEM((peers, per_dev, quarter), bf16),
            pltpu.VMEM((peers, per_dev, quarter), bf16),
            dma((chunks,)), dma((chunks,)), dma, dma, dma, dma((chunks,)), dma, dma((chunks,)),
            dma, dma,
        ],
        compiler_params=pltpu.CompilerParams(
            collective_id=0, has_side_effects=True, vmem_limit_bytes=56 << 20),
    )(expert_ids, tokens, router_weight.T, w_in, w_down)


def solution(mesh):
    rows = P(None, ("groups", "dp", "expert"), None)
    return jax.shard_map(
        functools.partial(body, mesh.shape["dp"], mesh.shape["expert"]),
        mesh=mesh,
        in_specs=(rows, rows, P(), P("dp", None, "expert"), P("expert", "dp")),
        out_specs=rows,
        check_vma=False,
    )
```

```python
import functools
import jax
import jax.numpy as jnp
from jax import lax
from jax.experimental import pallas as pl
from jax.experimental.pallas import tpu as pltpu
from jax.sharding import PartitionSpec as P

route_scale = 2.5
f32 = jnp.float32
bf16 = jnp.bfloat16


def loop(count, step):
    if count <= 32:
        for i in range(count):
            step(i)
    else:
        lax.fori_loop(0, count, lambda i, c: (step(i), c)[1], 0)


def kernel(n_dp, n_exp, ids, tok, rw, w_in, w_down, out, stage, xin, lhs, wv, dv, rs_out, r1,
           x_out, r2, h_all, acc, o_stage, ret, w_sem, d_sem, x_send, x_recv, r1_send, r1_recv,
           r2_send, r2_recv, hm_send, hm_recv, hx_send, hx_recv, hf_send, hf_recv, o_send, o_recv):
    num_micro, tok_rows, width = tok.shape
    top = ids.shape[2]
    experts = rw.shape[0]
    sharers = n_exp // experts
    quarter = width // n_dp
    per_dev = num_micro * tok_rows
    peers = n_dp * n_exp
    rows = peers * per_dev
    share = rows // n_dp
    chunks, _, cw = wv.shape
    assert n_dp == 4
    my_d = lax.axis_index("dp")
    my_z = lax.axis_index("expert")
    me = my_d * n_exp + my_z
    lo, hi = lax.rem(my_d, 2), my_d // 2
    mate, cross, far = 2 * hi + 1 - lo, 2 * (1 - hi) + lo, 2 * (1 - hi) + 1 - lo

    def w_copy(c):
        src = w_in.reshape(2 * quarter, chunks * cw)
        return pltpu.make_async_copy(src.at[:, pl.ds(c * cw, cw)], wv.at[c], w_sem.at[c])

    def d_copy(c):
        return pltpu.make_async_copy(w_down.at[pl.ds(c * cw, cw)], dv.at[c], d_sem.at[c])

    barrier = pltpu.get_barrier_semaphore()

    def peer_of(i):
        p = lax.rem(me + 1 + i, peers)
        return p, p // n_exp, lax.rem(p, n_exp)

    def greet(i):
        _, q, z = peer_of(i)
        pl.semaphore_signal(barrier, inc=1, device_id={"dp": q, "expert": z},
                            device_id_type=pl.DeviceIdType.MESH)

    loop(peers - 1, greet)
    for c in range(chunks):
        w_copy(c).start()
    for c in range(chunks):
        d_copy(c).start()
    mine = jnp.concatenate([tok[m].astype(f32) for m in range(num_micro)], axis=0)
    mine16 = mine.astype(bf16)
    for q in range(n_dp):
        stage[q] = mine16[:, q * quarter:(q + 1) * quarter]
    pl.semaphore_wait(barrier, peers - 1)

    def x_send_to(i):
        _, q, z = peer_of(i)
        pltpu.make_async_remote_copy(
            src_ref=stage.at[q], dst_ref=xin.at[me], send_sem=x_send, recv_sem=x_recv,
            device_id={"dp": q, "expert": z}, device_id_type=pl.DeviceIdType.MESH).start()

    loop(peers - 1, x_send_to)
    xin[me] = stage[my_d]
    logits = lax.dot_general(mine16, rw[...], (((1,), (1,)), ((), ())), preferred_element_type=f32)
    scores = 1.0 / (1.0 + jnp.exp(-logits))
    row = lax.broadcasted_iota(jnp.int32, (per_dev, experts), 0)
    col = lax.broadcasted_iota(jnp.int32, (per_dev, experts), 1)
    picked = jnp.zeros((per_dev, experts), f32)
    for m in range(num_micro):
        for t in range(tok_rows):
            for k in range(top):
                hit = (row == m * tok_rows + t) & (col == ids[m, t, k])
                picked = picked + jnp.where(hit, 1.0, 0.0)
    chosen = scores * picked
    gates = route_scale * chosen / jnp.sum(chosen, axis=1, keepdims=True)

    all_but_one = xin.at[pl.ds(0, peers - 1)]
    pltpu.make_async_copy(all_but_one, all_but_one, x_recv).wait()
    r_i = lax.broadcasted_iota(jnp.int32, (128, 256), 0)
    c_i = lax.broadcasted_iota(jnp.int32, (128, 256), 1)
    even = jnp.where(c_i == 2 * r_i, 1.0, 0.0).astype(bf16)
    odd = jnp.where(c_i == 2 * r_i + 1, 1.0, 0.0).astype(bf16)
    block = min(rows, 64)
    group = block // per_dev

    def expand(b):
        x = jnp.concatenate([xin[b * group + k].astype(f32) for k in range(group)], axis=0)
        x = x.astype(bf16)
        for j in range(quarter // 128):
            piece = x[:, j * 128:(j + 1) * 128]
            for s, spread in enumerate((even, odd)):
                lhs[s, pl.ds(b * block, block), pl.ds(j * 256, 256)] = jnp.dot(
                    piece, spread, preferred_element_type=f32).astype(bf16)

    if rows == block:
        expand(0)
    else:
        lax.fori_loop(0, rows // block, lambda b, c: (expand(b), c)[1], 0)

    def send(src, dst, send_sem, recv_sem, t):
        pltpu.make_async_remote_copy(
            src_ref=src, dst_ref=dst, send_sem=send_sem, recv_sem=recv_sem,
            device_id={"dp": t}, device_id_type=pl.DeviceIdType.MESH).start()

    def arrived(ref, sem):
        pltpu.make_async_copy(ref, ref, sem).wait()

    def up_chunk(c):
        w_copy(c).wait()
        if rows <= 64:
            res = jnp.dot(lhs[...].reshape(2 * rows, 2 * quarter), wv[c],
                          preferred_element_type=f32).astype(bf16)
            for t in range(n_dp):
                for s in range(2):
                    rs_out[c, t % 2, t // 2, s] = res[s * rows + t * share:
                                                      s * rows + (t + 1) * share]
        else:
            per = share // block

            def part(b, carry):
                src = pl.ds(pl.multiple_of(b * block, block), block)
                at = pl.ds(pl.multiple_of(lax.rem(b, per) * block, block), block)
                t = b // per
                for s in range(2):
                    rs_out[c, lax.rem(t, 2), t // 2, s, at] = jnp.dot(
                        lhs[s, src], wv[c], preferred_element_type=f32).astype(bf16)
                return carry
            lax.fori_loop(0, rows // block, part, 0)
        send(rs_out.at[c, 1 - lo], r1.at[c], r1_send, r1_recv.at[c], mate)

    def pair_chunk(c):
        arrived(r1.at[c], r1_recv.at[c])
        x_out[c] = (rs_out[c, lo, 1 - hi].astype(f32) + r1[c, 1 - hi].astype(f32)).astype(bf16)
        send(x_out.at[c], r2.at[c], r2_send, r2_recv.at[c], cross)

    def hidden_chunk(c):
        own = rs_out[c, lo, hi].astype(f32) + r1[c, hi].astype(f32)
        arrived(r2.at[c], r2_recv.at[c])
        total = own + r2[c].astype(f32)
        gate, up = total[0], total[1]
        h_all[c, my_d] = (gate / (1.0 + jnp.exp(-gate)) * up).astype(bf16)
        here = h_all.at[c, my_d]
        send(here, here, hx_send, hx_recv.at[c], cross)
        send(here, here, hm_send, hm_recv.at[c], mate)

    def forward_chunk(c):
        there = h_all.at[c, cross]
        arrived(there, hx_recv.at[c])
        send(there, there, hf_send, hf_recv.at[c], mate)

    def down_chunk(c):
        d_copy(c).wait()
        arrived(h_all.at[c, mate], hm_recv.at[c])
        arrived(h_all.at[c, far], hf_recv.at[c])
        if rows <= 64:
            part = jnp.dot(h_all[c].reshape(rows, cw), dv[c], preferred_element_type=f32)
            acc[...] = part if c == 0 else acc[...] + part
        else:
            per = share // block

            def part(b, carry):
                src = pl.ds(pl.multiple_of(lax.rem(b, per) * block, block), block)
                at = pl.ds(pl.multiple_of(b * block, block), block)
                value = jnp.dot(h_all[c, b // per, src], dv[c], preferred_element_type=f32)
                acc[at] = value if c == 0 else acc[at] + value
                return carry
            lax.fori_loop(0, rows // block, part, 0)

    stages = ((0, up_chunk), (2, pair_chunk), (4, hidden_chunk), (6, forward_chunk), (8, down_chunk))
    for step in range(chunks + stages[-1][0]):
        for lag, stage_of in stages:
            if 0 <= step - lag < chunks:
                stage_of(step - lag)

    def spread_out(i):
        v = acc[pl.ds(i * 16, 16), :]
        for k in range(16 // per_dev):
            o_stage[i * (16 // per_dev) + k] = v[k * per_dev:(k + 1) * per_dev].astype(bf16)

    loop(rows // 16, spread_out)

    def o_send_to(i):
        p, q, z = peer_of(i)
        pltpu.make_async_remote_copy(
            src_ref=o_stage.at[p], dst_ref=ret.at[me], send_sem=o_send, recv_sem=o_recv,
            device_id={"dp": q, "expert": z}, device_id_type=pl.DeviceIdType.MESH).start()

    loop(peers - 1, o_send_to)
    ret[me] = o_stage[me]
    back = ret.at[pl.ds(0, peers - 1)]
    pltpu.make_async_copy(back, back, o_recv).wait()
    for q in range(n_dp):
        total = jnp.zeros((per_dev, quarter), f32)
        for e in range(experts):
            part = ret[q * n_exp + e * sharers].astype(f32)
            for s in range(1, sharers):
                part = part + ret[q * n_exp + e * sharers + s].astype(f32)
            total = total + gates[:, e:e + 1] * part
        for m in range(num_micro):
            out[m, :, pl.ds(q * quarter, quarter)] = total[
                m * tok_rows:(m + 1) * tok_rows].astype(bf16)
    pltpu.make_async_copy(all_but_one, all_but_one, x_send).wait()
    arrived(r1, r1_send)
    arrived(r2, r2_send)
    for sem in (hm_send, hx_send, hf_send):
        arrived(h_all.at[:, 0], sem)
    pltpu.make_async_copy(back, back, o_send).wait()


def body(n_dp, n_exp, tokens, expert_ids, router_weight, w_in, w_down):
    num_micro, tok_rows, width = tokens.shape
    quarter, _, ff = w_in.shape
    per_dev = num_micro * tok_rows
    peers = n_dp * n_exp
    rows = peers * per_dev
    share = rows // n_dp
    cw = min(256, ff)
    chunks = ff // cw
    vmem = pl.BlockSpec(memory_space=pltpu.VMEM)
    dma = pltpu.SemaphoreType.DMA
    return pl.pallas_call(
        functools.partial(kernel, n_dp, n_exp),
        out_shape=jax.ShapeDtypeStruct(tokens.shape, bf16),
        in_specs=[pl.BlockSpec(memory_space=pltpu.SMEM), vmem, vmem,
                  pl.BlockSpec(memory_space=pl.ANY), pl.BlockSpec(memory_space=pl.ANY)],
        out_specs=vmem,
        scratch_shapes=[
            pltpu.VMEM((n_dp, per_dev, quarter), bf16),
            pltpu.VMEM((peers, per_dev, quarter), bf16),
            pltpu.VMEM((2, rows, 2 * quarter), bf16),
            pltpu.VMEM((chunks, 2 * quarter, cw), bf16),
            pltpu.VMEM((chunks, cw, quarter), bf16),
            pltpu.VMEM((chunks, 2, 2, 2, share, cw), bf16),
            pltpu.VMEM((chunks, 2, 2, share, cw), bf16),
            pltpu.VMEM((chunks, 2, share, cw), bf16),
            pltpu.VMEM((chunks, 2, share, cw), bf16),
            pltpu.VMEM((chunks, n_dp, share, cw), bf16),
            pltpu.VMEM((rows, quarter), f32),
            pltpu.VMEM((peers, per_dev, quarter), bf16),
            pltpu.VMEM((peers, per_dev, quarter), bf16),
            dma((chunks,)), dma((chunks,)), dma, dma, dma, dma((chunks,)), dma, dma((chunks,)),
            dma, dma((chunks,)), dma, dma((chunks,)), dma, dma((chunks,)), dma, dma,
        ],
        compiler_params=pltpu.CompilerParams(
            collective_id=0, has_side_effects=True, vmem_limit_bytes=56 << 20),
    )(expert_ids, tokens, router_weight.T, w_in, w_down)


def solution(mesh):
    rows = P(None, ("groups", "dp", "expert"), None)
    return jax.shard_map(
        functools.partial(body, mesh.shape["dp"], mesh.shape["expert"]),
        mesh=mesh,
        in_specs=(rows, rows, P(), P("dp", None, "expert"), P("expert", "dp")),
        out_specs=rows,
        check_vma=False,
    )
```

```python
import functools
import jax
import jax.numpy as jnp
from jax import lax
from jax.experimental import pallas as pl
from jax.experimental.pallas import tpu as pltpu
from jax.sharding import PartitionSpec as P

route_scale = 2.5
f32 = jnp.float32
bf16 = jnp.bfloat16


def loop(count, step):
    if count <= 32:
        for i in range(count):
            step(i)
    else:
        lax.fori_loop(0, count, lambda i, c: (step(i), c)[1], 0)


def kernel(n_dp, n_exp, ids, tok, rw, w_in, w_down, out, stage, xin, lhs, wv, dv, rs_out, rs_in,
           h_all, acc, o_stage, ret, w_sem, d_sem, x_send, x_recv, rs_send, rs_recv, h_send,
           h_recv, o_send, o_recv):
    num_micro, tok_rows, width = tok.shape
    top = ids.shape[2]
    experts = rw.shape[0]
    sharers = n_exp // experts
    quarter = width // n_dp
    per_dev = num_micro * tok_rows
    peers = n_dp * n_exp
    rows = peers * per_dev
    share = rows // n_dp
    chunks, _, cw = wv.shape
    my_d = lax.axis_index("dp")
    my_z = lax.axis_index("expert")
    me = my_d * n_exp + my_z

    def w_copy(c):
        src = w_in.reshape(2 * quarter, chunks * cw)
        return pltpu.make_async_copy(src.at[:, pl.ds(c * cw, cw)], wv.at[c], w_sem.at[c])

    def d_copy(c):
        return pltpu.make_async_copy(w_down.at[pl.ds(c * cw, cw)], dv.at[c], d_sem.at[c])

    barrier = pltpu.get_barrier_semaphore()

    def peer_of(i):
        p = lax.rem(me + 1 + i, peers)
        return p, p // n_exp, lax.rem(p, n_exp)

    def greet(i):
        _, q, z = peer_of(i)
        pl.semaphore_signal(barrier, inc=1, device_id={"dp": q, "expert": z},
                            device_id_type=pl.DeviceIdType.MESH)

    loop(peers - 1, greet)
    for c in range(chunks):
        w_copy(c).start()
    for c in range(chunks):
        d_copy(c).start()
    mine = jnp.concatenate([tok[m].astype(f32) for m in range(num_micro)], axis=0)
    mine16 = mine.astype(bf16)
    for q in range(n_dp):
        stage[q] = mine16[:, q * quarter:(q + 1) * quarter]
    pl.semaphore_wait(barrier, peers - 1)

    def x_send_to(i):
        _, q, z = peer_of(i)
        pltpu.make_async_remote_copy(
            src_ref=stage.at[q], dst_ref=xin.at[me], send_sem=x_send, recv_sem=x_recv,
            device_id={"dp": q, "expert": z}, device_id_type=pl.DeviceIdType.MESH).start()

    loop(peers - 1, x_send_to)
    xin[me] = stage[my_d]
    logits = lax.dot_general(mine16, rw[...], (((1,), (1,)), ((), ())), preferred_element_type=f32)
    scores = 1.0 / (1.0 + jnp.exp(-logits))
    row = lax.broadcasted_iota(jnp.int32, (per_dev, experts), 0)
    col = lax.broadcasted_iota(jnp.int32, (per_dev, experts), 1)
    picked = jnp.zeros((per_dev, experts), f32)
    for m in range(num_micro):
        for t in range(tok_rows):
            for k in range(top):
                hit = (row == m * tok_rows + t) & (col == ids[m, t, k])
                picked = picked + jnp.where(hit, 1.0, 0.0)
    chosen = scores * picked
    gates = route_scale * chosen / jnp.sum(chosen, axis=1, keepdims=True)

    all_but_one = xin.at[pl.ds(0, peers - 1)]
    pltpu.make_async_copy(all_but_one, all_but_one, x_recv).wait()
    r_i = lax.broadcasted_iota(jnp.int32, (128, 256), 0)
    c_i = lax.broadcasted_iota(jnp.int32, (128, 256), 1)
    even = jnp.where(c_i == 2 * r_i, 1.0, 0.0).astype(bf16)
    odd = jnp.where(c_i == 2 * r_i + 1, 1.0, 0.0).astype(bf16)
    block = min(rows, 64)
    group = block // per_dev

    def expand(b):
        x = jnp.concatenate([xin[b * group + k].astype(f32) for k in range(group)], axis=0)
        x = x.astype(bf16)
        for j in range(quarter // 128):
            piece = x[:, j * 128:(j + 1) * 128]
            for s, spread in enumerate((even, odd)):
                lhs[s, pl.ds(b * block, block), pl.ds(j * 256, 256)] = jnp.dot(
                    piece, spread, preferred_element_type=f32).astype(bf16)

    if rows == block:
        expand(0)
    else:
        lax.fori_loop(0, rows // block, lambda b, c: (expand(b), c)[1], 0)

    def up_chunk(c):
        w_copy(c).wait()
        if rows <= 64:
            res = jnp.dot(lhs[...].reshape(2 * rows, 2 * quarter), wv[c],
                          preferred_element_type=f32).astype(bf16)
            rs_out[c] = res.reshape(2, rows, cw)
        else:
            def part(b, carry):
                at = pl.ds(pl.multiple_of(b * block, block), block)
                for s in range(2):
                    rs_out[c, s, at] = jnp.dot(lhs[s, at], wv[c],
                                               preferred_element_type=f32).astype(bf16)
                return carry
            lax.fori_loop(0, rows // block, part, 0)
        for o in range(1, n_dp):
            t = lax.rem(my_d + o, n_dp)
            pltpu.make_async_remote_copy(
                src_ref=rs_out.at[c, :, pl.ds(pl.multiple_of(t * share, share), share)],
                dst_ref=rs_in.at[c, n_dp - 1 - o], send_sem=rs_send, recv_sem=rs_recv.at[c],
                device_id={"dp": t}, device_id_type=pl.DeviceIdType.MESH).start()

    def hidden_chunk(c):
        pltpu.make_async_copy(rs_in.at[c], rs_in.at[c], rs_recv.at[c]).wait()
        at = pl.ds(pl.multiple_of(my_d * share, share), share)
        total = rs_out[c, :, at].astype(f32)
        for o in range(n_dp - 1):
            total = total + rs_in[c, o].astype(f32)
        gate, up = total[0], total[1]
        h_all[c, my_d] = (gate / (1.0 + jnp.exp(-gate)) * up).astype(bf16)
        for o in range(1, n_dp):
            t = lax.rem(my_d + o, n_dp)
            pltpu.make_async_remote_copy(
                src_ref=h_all.at[c, my_d], dst_ref=h_all.at[c, my_d], send_sem=h_send,
                recv_sem=h_recv.at[c], device_id={"dp": t},
                device_id_type=pl.DeviceIdType.MESH).start()

    def down_chunk(c):
        d_copy(c).wait()
        others = h_all.at[c, pl.ds(0, n_dp - 1)]
        pltpu.make_async_copy(others, others, h_recv.at[c]).wait()
        if rows <= 64:
            part = jnp.dot(h_all[c].reshape(rows, cw), dv[c], preferred_element_type=f32)
            acc[...] = part if c == 0 else acc[...] + part
        else:
            per = share // block

            def part(b, carry):
                src = pl.ds(pl.multiple_of(lax.rem(b, per) * block, block), block)
                at = pl.ds(pl.multiple_of(b * block, block), block)
                value = jnp.dot(h_all[c, b // per, src], dv[c], preferred_element_type=f32)
                acc[at] = value if c == 0 else acc[at] + value
                return carry
            lax.fori_loop(0, rows // block, part, 0)

    lag_h, lag_d = chunks, 2 * chunks
    for step in range(chunks + lag_d):
        if step < chunks:
            up_chunk(step)
        if 0 <= step - lag_h < chunks:
            hidden_chunk(step - lag_h)
        if 0 <= step - lag_d < chunks:
            down_chunk(step - lag_d)

    per_step = 16 // per_dev

    def spread_out(i):
        v = acc[pl.ds(i * 16, 16), :]
        for k in range(per_step):
            p = i * per_step + k
            o_stage[p] = v[k * per_dev:(k + 1) * per_dev].astype(bf16)

            @pl.when(p != me)
            def _():
                pltpu.make_async_remote_copy(
                    src_ref=o_stage.at[p], dst_ref=ret.at[me], send_sem=o_send, recv_sem=o_recv,
                    device_id={"dp": p // n_exp, "expert": p % n_exp},
                    device_id_type=pl.DeviceIdType.MESH).start()

    loop(rows // 16, spread_out)
    ret[me] = o_stage[me]
    back = ret.at[pl.ds(0, peers - 1)]
    pltpu.make_async_copy(back, back, o_recv).wait()
    for q in range(n_dp):
        total = jnp.zeros((per_dev, quarter), f32)
        for e in range(experts):
            part = ret[q * n_exp + e * sharers].astype(f32)
            for s in range(1, sharers):
                part = part + ret[q * n_exp + e * sharers + s].astype(f32)
            total = total + gates[:, e:e + 1] * part
        for m in range(num_micro):
            out[m, :, pl.ds(q * quarter, quarter)] = total[
                m * tok_rows:(m + 1) * tok_rows].astype(bf16)
    pltpu.make_async_copy(all_but_one, all_but_one, x_send).wait()
    pltpu.make_async_copy(rs_in, rs_in, rs_send).wait()
    sent = h_all.at[:, pl.ds(0, n_dp - 1)]
    pltpu.make_async_copy(sent, sent, h_send).wait()
    pltpu.make_async_copy(back, back, o_send).wait()


def body(n_dp, n_exp, tokens, expert_ids, router_weight, w_in, w_down):
    num_micro, tok_rows, width = tokens.shape
    quarter, _, ff = w_in.shape
    per_dev = num_micro * tok_rows
    peers = n_dp * n_exp
    rows = peers * per_dev
    share = rows // n_dp
    cw = min(256, ff)
    chunks = ff // cw
    vmem = pl.BlockSpec(memory_space=pltpu.VMEM)
    dma = pltpu.SemaphoreType.DMA
    return pl.pallas_call(
        functools.partial(kernel, n_dp, n_exp),
        out_shape=jax.ShapeDtypeStruct(tokens.shape, bf16),
        in_specs=[pl.BlockSpec(memory_space=pltpu.SMEM), vmem, vmem,
                  pl.BlockSpec(memory_space=pl.ANY), pl.BlockSpec(memory_space=pl.ANY)],
        out_specs=vmem,
        scratch_shapes=[
            pltpu.VMEM((n_dp, per_dev, quarter), bf16),
            pltpu.VMEM((peers, per_dev, quarter), bf16),
            pltpu.VMEM((2, rows, 2 * quarter), bf16),
            pltpu.VMEM((chunks, 2 * quarter, cw), bf16),
            pltpu.VMEM((chunks, cw, quarter), bf16),
            pltpu.VMEM((chunks, 2, rows, cw), bf16),
            pltpu.VMEM((chunks, n_dp - 1, 2, share, cw), bf16),
            pltpu.VMEM((chunks, n_dp, share, cw), bf16),
            pltpu.VMEM((rows, quarter), f32),
            pltpu.VMEM((peers, per_dev, quarter), bf16),
            pltpu.VMEM((peers, per_dev, quarter), bf16),
            dma((chunks,)), dma((chunks,)), dma, dma, dma, dma((chunks,)), dma, dma((chunks,)),
            dma, dma,
        ],
        compiler_params=pltpu.CompilerParams(
            collective_id=0, has_side_effects=True, vmem_limit_bytes=56 << 20),
    )(expert_ids, tokens, router_weight.T, w_in, w_down)


def solution(mesh):
    rows = P(None, ("groups", "dp", "expert"), None)
    return jax.shard_map(
        functools.partial(body, mesh.shape["dp"], mesh.shape["expert"]),
        mesh=mesh,
        in_specs=(rows, rows, P(), P("dp", None, "expert"), P("expert", "dp")),
        out_specs=rows,
        check_vma=False,
    )
```

```python
import functools
import jax
import jax.numpy as jnp
from jax import lax
from jax.experimental import pallas as pl
from jax.experimental.pallas import tpu as pltpu
from jax.sharding import PartitionSpec as P

route_scale = 2.5
f32 = jnp.float32
bf16 = jnp.bfloat16


def loop(count, step):
    if count <= 32:
        for i in range(count):
            step(i)
    else:
        lax.fori_loop(0, count, lambda i, c: (step(i), c)[1], 0)


def kernel(n_dp, n_exp, ids, tok, rw, w_in, w_down, out, stage, xin, lhs, wv, dv, rs_out, rs_in,
           h_all, acc, o_stage, ret, w_sem, d_sem, x_send, x_recv, rs_send, rs_recv, h_send,
           h_recv, o_send, o_recv):
    num_micro, tok_rows, width = tok.shape
    top = ids.shape[2]
    experts = rw.shape[0]
    sharers = n_exp // experts
    quarter = width // n_dp
    per_dev = num_micro * tok_rows
    peers = n_dp * n_exp
    rows = peers * per_dev
    share = rows // n_dp
    chunks, _, cw = wv.shape
    my_d = lax.axis_index("dp")
    my_z = lax.axis_index("expert")
    me = my_d * n_exp + my_z

    def w_copy(c):
        src = w_in.reshape(2 * quarter, chunks * cw)
        return pltpu.make_async_copy(src.at[:, pl.ds(c * cw, cw)], wv.at[c], w_sem.at[c])

    def d_copy(c):
        return pltpu.make_async_copy(w_down.at[pl.ds(c * cw, cw)], dv.at[c], d_sem.at[c])

    barrier = pltpu.get_barrier_semaphore()

    def peer_of(i):
        p = lax.rem(me + 1 + i, peers)
        return p, p // n_exp, lax.rem(p, n_exp)

    def greet(i):
        _, q, z = peer_of(i)
        pl.semaphore_signal(barrier, inc=1, device_id={"dp": q, "expert": z},
                            device_id_type=pl.DeviceIdType.MESH)

    loop(peers - 1, greet)
    for c in range(chunks):
        w_copy(c).start()
    for c in range(chunks):
        d_copy(c).start()
    mine = jnp.concatenate([tok[m].astype(f32) for m in range(num_micro)], axis=0)
    mine16 = mine.astype(bf16)
    for q in range(n_dp):
        stage[q] = mine16[:, q * quarter:(q + 1) * quarter]
    pl.semaphore_wait(barrier, peers - 1)

    def x_send_to(i):
        _, q, z = peer_of(i)
        pltpu.make_async_remote_copy(
            src_ref=stage.at[q], dst_ref=xin.at[me], send_sem=x_send, recv_sem=x_recv,
            device_id={"dp": q, "expert": z}, device_id_type=pl.DeviceIdType.MESH).start()

    loop(peers - 1, x_send_to)
    xin[me] = stage[my_d]
    logits = lax.dot_general(mine16, rw[...], (((1,), (1,)), ((), ())), preferred_element_type=f32)
    scores = 1.0 / (1.0 + jnp.exp(-logits))
    row = lax.broadcasted_iota(jnp.int32, (per_dev, experts), 0)
    col = lax.broadcasted_iota(jnp.int32, (per_dev, experts), 1)
    picked = jnp.zeros((per_dev, experts), f32)
    for m in range(num_micro):
        for t in range(tok_rows):
            for k in range(top):
                hit = (row == m * tok_rows + t) & (col == ids[m, t, k])
                picked = picked + jnp.where(hit, 1.0, 0.0)
    chosen = scores * picked
    gates = route_scale * chosen / jnp.sum(chosen, axis=1, keepdims=True)

    all_but_one = xin.at[pl.ds(0, peers - 1)]
    pltpu.make_async_copy(all_but_one, all_but_one, x_recv).wait()
    r_i = lax.broadcasted_iota(jnp.int32, (128, 256), 0)
    c_i = lax.broadcasted_iota(jnp.int32, (128, 256), 1)
    even = jnp.where(c_i == 2 * r_i, 1.0, 0.0).astype(bf16)
    odd = jnp.where(c_i == 2 * r_i + 1, 1.0, 0.0).astype(bf16)
    block = min(rows, 64)
    group = block // per_dev

    def expand(b):
        x = jnp.concatenate([xin[b * group + k].astype(f32) for k in range(group)], axis=0)
        x = x.astype(bf16)
        for j in range(quarter // 128):
            piece = x[:, j * 128:(j + 1) * 128]
            for s, spread in enumerate((even, odd)):
                lhs[s, pl.ds(b * block, block), pl.ds(j * 256, 256)] = jnp.dot(
                    piece, spread, preferred_element_type=f32).astype(bf16)

    if rows == block:
        expand(0)
    else:
        lax.fori_loop(0, rows // block, lambda b, c: (expand(b), c)[1], 0)

    def up_chunk(c):
        w_copy(c).wait()
        if rows <= 64:
            res = jnp.dot(lhs[...].reshape(2 * rows, 2 * quarter), wv[c],
                          preferred_element_type=f32).astype(bf16)
            rs_out[c] = res.reshape(2, rows, cw)
        else:
            def part(b, carry):
                at = pl.ds(pl.multiple_of(b * block, block), block)
                for s in range(2):
                    rs_out[c, s, at] = jnp.dot(lhs[s, at], wv[c],
                                               preferred_element_type=f32).astype(bf16)
                return carry
            lax.fori_loop(0, rows // block, part, 0)
        for o in (*range(2, n_dp), 1):
            t = lax.rem(my_d + o, n_dp)
            pltpu.make_async_remote_copy(
                src_ref=rs_out.at[c, :, pl.ds(pl.multiple_of(t * share, share), share)],
                dst_ref=rs_in.at[c, n_dp - 1 - o], send_sem=rs_send, recv_sem=rs_recv.at[c],
                device_id={"dp": t}, device_id_type=pl.DeviceIdType.MESH).start()

    def hidden_chunk(c):
        pltpu.make_async_copy(rs_in.at[c], rs_in.at[c], rs_recv.at[c]).wait()
        at = pl.ds(pl.multiple_of(my_d * share, share), share)
        total = rs_out[c, :, at].astype(f32)
        for o in range(n_dp - 1):
            total = total + rs_in[c, o].astype(f32)
        gate, up = total[0], total[1]
        h_all[c, my_d] = (gate / (1.0 + jnp.exp(-gate)) * up).astype(bf16)
        for o in (*range(2, n_dp), 1):
            t = lax.rem(my_d + o, n_dp)
            pltpu.make_async_remote_copy(
                src_ref=h_all.at[c, my_d], dst_ref=h_all.at[c, my_d], send_sem=h_send,
                recv_sem=h_recv.at[c], device_id={"dp": t},
                device_id_type=pl.DeviceIdType.MESH).start()

    def down_chunk(c):
        d_copy(c).wait()
        others = h_all.at[c, pl.ds(0, n_dp - 1)]
        pltpu.make_async_copy(others, others, h_recv.at[c]).wait()
        if rows <= 64:
            part = jnp.dot(h_all[c].reshape(rows, cw), dv[c], preferred_element_type=f32)
            acc[...] = part if c == 0 else acc[...] + part
        else:
            per = share // block

            def part(b, carry):
                src = pl.ds(pl.multiple_of(lax.rem(b, per) * block, block), block)
                at = pl.ds(pl.multiple_of(b * block, block), block)
                value = jnp.dot(h_all[c, b // per, src], dv[c], preferred_element_type=f32)
                acc[at] = value if c == 0 else acc[at] + value
                return carry
            lax.fori_loop(0, rows // block, part, 0)

    lag_h, lag_d = chunks, 2 * chunks
    for step in range(chunks + lag_d):
        if step < chunks:
            up_chunk(step)
        if 0 <= step - lag_h < chunks:
            hidden_chunk(step - lag_h)
        if 0 <= step - lag_d < chunks:
            down_chunk(step - lag_d)

    per_step = 16 // per_dev

    def spread_out(i):
        v = acc[pl.ds(i * 16, 16), :]
        for k in range(per_step):
            p = i * per_step + k
            o_stage[p] = v[k * per_dev:(k + 1) * per_dev].astype(bf16)

            @pl.when(p != me)
            def _():
                pltpu.make_async_remote_copy(
                    src_ref=o_stage.at[p], dst_ref=ret.at[me], send_sem=o_send, recv_sem=o_recv,
                    device_id={"dp": p // n_exp, "expert": p % n_exp},
                    device_id_type=pl.DeviceIdType.MESH).start()

    loop(rows // 16, spread_out)
    ret[me] = o_stage[me]
    back = ret.at[pl.ds(0, peers - 1)]
    pltpu.make_async_copy(back, back, o_recv).wait()
    for q in range(n_dp):
        total = jnp.zeros((per_dev, quarter), f32)
        for e in range(experts):
            part = ret[q * n_exp + e * sharers].astype(f32)
            for s in range(1, sharers):
                part = part + ret[q * n_exp + e * sharers + s].astype(f32)
            total = total + gates[:, e:e + 1] * part
        for m in range(num_micro):
            out[m, :, pl.ds(q * quarter, quarter)] = total[
                m * tok_rows:(m + 1) * tok_rows].astype(bf16)
    pltpu.make_async_copy(all_but_one, all_but_one, x_send).wait()
    pltpu.make_async_copy(rs_in, rs_in, rs_send).wait()
    sent = h_all.at[:, pl.ds(0, n_dp - 1)]
    pltpu.make_async_copy(sent, sent, h_send).wait()
    pltpu.make_async_copy(back, back, o_send).wait()


def body(n_dp, n_exp, tokens, expert_ids, router_weight, w_in, w_down):
    num_micro, tok_rows, width = tokens.shape
    quarter, _, ff = w_in.shape
    per_dev = num_micro * tok_rows
    peers = n_dp * n_exp
    rows = peers * per_dev
    share = rows // n_dp
    cw = min(512, ff)
    chunks = ff // cw
    vmem = pl.BlockSpec(memory_space=pltpu.VMEM)
    dma = pltpu.SemaphoreType.DMA
    return pl.pallas_call(
        functools.partial(kernel, n_dp, n_exp),
        out_shape=jax.ShapeDtypeStruct(tokens.shape, bf16),
        in_specs=[pl.BlockSpec(memory_space=pltpu.SMEM), vmem, vmem,
                  pl.BlockSpec(memory_space=pl.ANY), pl.BlockSpec(memory_space=pl.ANY)],
        out_specs=vmem,
        scratch_shapes=[
            pltpu.VMEM((n_dp, per_dev, quarter), bf16),
            pltpu.VMEM((peers, per_dev, quarter), bf16),
            pltpu.VMEM((2, rows, 2 * quarter), bf16),
            pltpu.VMEM((chunks, 2 * quarter, cw), bf16),
            pltpu.VMEM((chunks, cw, quarter), bf16),
            pltpu.VMEM((chunks, 2, rows, cw), bf16),
            pltpu.VMEM((chunks, n_dp - 1, 2, share, cw), bf16),
            pltpu.VMEM((chunks, n_dp, share, cw), bf16),
            pltpu.VMEM((rows, quarter), f32),
            pltpu.VMEM((peers, per_dev, quarter), bf16),
            pltpu.VMEM((peers, per_dev, quarter), bf16),
            dma((chunks,)), dma((chunks,)), dma, dma, dma, dma((chunks,)), dma, dma((chunks,)),
            dma, dma,
        ],
        compiler_params=pltpu.CompilerParams(
            collective_id=0, has_side_effects=True, vmem_limit_bytes=56 << 20),
    )(expert_ids, tokens, router_weight.T, w_in, w_down)


def solution(mesh):
    rows = P(None, ("groups", "dp", "expert"), None)
    return jax.shard_map(
        functools.partial(body, mesh.shape["dp"], mesh.shape["expert"]),
        mesh=mesh,
        in_specs=(rows, rows, P(), P("dp", None, "expert"), P("expert", "dp")),
        out_specs=rows,
        check_vma=False,
    )
```
